128 devices in a mesh: frame: 16 (over x_lo, z, core), head: 8 (over y, x_hi).
Axes of the slice: x: 4 (x_hi: 2, x_lo: 2; x = x_hi * 2 + x_lo), y: 4, z: 4, core: 2. Of those that a mesh axis runs over, the one named last changes fastest.
Arguments:
- queries: bfloat16 [1024, 8192], P('frame', 'head'), may hold values from -6 to 6
- q_gain: float32 [128], replicated, may hold values from 0.1 to 1.9
- keys: bfloat16 [25600, 1024], P('frame', 'head'), may hold values from -6 to 6
- k_gain: float32 [128], replicated, may hold values from 0.1 to 1.9
- values: bfloat16 [25600, 1024], P('frame', 'head'), may hold values from -6 to 6
- out_grad: bfloat16 [1024, 8192], P('frame', 'head'), may hold values from -384 to 384
- w_query: bfloat16 [8192, 8192], P(None, 'head'), may hold values from -0.0625 to 0.0625
- span_mask: int32 [64, 16], P(None, 'frame'), may hold values from 0 to 1, as said below
- frame_len: int32 [16], P('frame'), may hold values from 400 to 1600
Outputs:
- text_grad: float32 [1024, 8192], P('frame', 'head')
- key_grad: float32 [25600, 1024], P('frame', 'head')
- value_grad: float32 [25600, 1024], P('frame', 'head')
The draws below stay inside these ranges and needn't reach their ends.
Inputs may be any that keep to these rules, and one draw needn't show every extreme that they name: `span_mask`: every text span sees at least one frame.
All inputs are finite; a program needn't handle non-finite values.
Results may differ from the reference program's by a relative error of at most 0.012.
The reference program's roundings to bfloat16 on the way (of `qb`, `kb` and `dq`) count: a program that leaves them out, or rounds other values in their place, can miss the bound.
Values may be sent and summed in bfloat16 or wider, within the bound.
A program may use at most 128 MiB of HBM per device.

```python
import jax
import jax.numpy as jnp
from jax import lax

D = 8192
QH = 64
KVH = 8
HD = 128
KF = 1600
BLK = 16
TXT = 1024
FRAMES = 16
KEYS = 25600
SPANS = 64


def draw_span_mask(key, part):
    key_level, key_bits, key_pick = jax.random.split(key, 3)
    level = jax.random.randint(key_level, (1, FRAMES), 1, 5)
    bits = jax.random.randint(key_bits, (SPANS, FRAMES), 0, 4) < level
    pick = jax.random.randint(key_pick, (SPANS, 1), 0, FRAMES)
    chosen = pick == jnp.arange(FRAMES, dtype=jnp.int32)[None, :]
    return (bits | chosen).astype(jnp.int32)


def touch_ends(array, key, least, high):
    longest = array.shape.index(max(array.shape))
    spots = []
    for shift in (0, 1):
        where = [jax.random.randint(jax.random.fold_in(key, axis), (), 0, length) for axis, length in enumerate(array.shape)]
        where[longest] = (where[longest] + shift) % array.shape[longest]
        spots.append(tuple(where))
    return array.at[spots[0]].set(least).at[spots[1]].set(high)


def steps_of(key, extent, cuts, least, largest):
    level, own = 1.0, jax.random.fold_in(key, 6)
    for position, blocks in cuts:
        heights = jnp.exp(jax.random.uniform(jax.random.fold_in(own, position), (blocks,), jnp.float32, least / len(cuts), largest / len(cuts)))
        level = level * jnp.repeat(heights, extent[position] // blocks).reshape([-1 if axis == position else 1 for axis in range(len(extent))])
    return level


def normal_values(stream_key, dims, width, reach, pieces=(), kind=jnp.bfloat16):
    entries = jax.random.normal(stream_key, dims, jnp.float32) * width
    if len(pieces) > 0:
        entries = steps_of(stream_key, dims, pieces, -0.22, 0.18) * entries
    return jnp.clip(entries, min=-reach, max=reach).astype(kind)


def setup_inputs(seed: int = 0) -> dict:
    streams_of = jax.random.split(jax.random.key(seed), 10)
    queries = normal_values(streams_of[0], (TXT, QH * HD), 1.0, 6.0, ((0, 16), (1, 8)))
    q_gain = jnp.clip(1.0 + 0.18 * jax.random.normal(streams_of[1], (HD,), jnp.float32), 0.1, 1.9)
    keys = normal_values(streams_of[2], (KEYS, KVH * HD), 1.0, 6.0, ((0, 16), (1, 8)))
    k_gain = jnp.clip(1.0 + 0.18 * jax.random.normal(streams_of[3], (HD,), jnp.float32), 0.1, 1.9)
    values = normal_values(streams_of[4], (KEYS, KVH * HD), 1.0, 6.0, ((0, 16), (1, 8)))
    out_grad = normal_values(streams_of[5], (TXT, QH * HD), 64.0, 384.0, ((0, 16), (1, 8)))
    w_query = normal_values(streams_of[6], (D, QH * HD), D ** -0.5, 0.0625, ((1, 8),))
    span_mask = draw_span_mask(jax.random.fold_in(streams_of[9], 71), 0)
    frame_len = touch_ends(jax.random.randint(streams_of[8], (FRAMES,), KF // 4, KF + 1), jax.random.fold_in(streams_of[8], 1), KF // 4, KF).astype(jnp.int32)
    return {"queries": queries, "q_gain": q_gain, "keys": keys, "k_gain": k_gain, "values": values, "out_grad": out_grad, "w_query": w_query, "span_mask": span_mask, "frame_len": frame_len}


EPS = 1e-05

def reference(queries, q_gain, keys, k_gain, values, out_grad, w_query, span_mask, frame_len):
    group = QH // KVH
    q = queries.astype(jnp.float32).reshape(TXT, QH, HD)
    rq = lax.rsqrt(lax.optimization_barrier(jnp.mean(q * q, axis=-1, keepdims=True)) + EPS)
    qb = (q * rq * q_gain * HD ** (-0.5)).astype(jnp.bfloat16)
    k = keys.astype(jnp.float32).reshape(KEYS, KVH, HD)
    rk = lax.rsqrt(lax.optimization_barrier(jnp.mean(k * k, axis=-1, keepdims=True)) + EPS)
    kb = (k * rk * k_gain).astype(jnp.bfloat16)
    key_pos = jnp.arange(KEYS)
    frame_of = key_pos // KF
    key_ok = key_pos % KF < frame_len[frame_of]
    span_of = jnp.arange(TXT) // BLK
    visible = (span_mask[span_of][:, frame_of] > 0) & key_ok[None, :]
    q_groups = qb.reshape(TXT, KVH, group, HD).transpose(1, 2, 0, 3)
    d_groups = out_grad.reshape(TXT, KVH, group, HD).transpose(1, 2, 0, 3)
    k_groups = kb.transpose(1, 0, 2)
    v_groups = values.reshape(KEYS, KVH, HD).transpose(1, 0, 2)

    def per_kv(items):
        q_heads, d_heads, k_head, v_head = items

        def per_head(carry, pair):
            dk_acc, dv_acc = carry
            q_one, d_one = pair
            scores = jnp.dot(q_one, k_head.T, preferred_element_type=jnp.float32)
            expd = jnp.where(visible, jnp.exp(scores), jnp.float32(0.0))
            dprob = jnp.dot(d_one, v_head.T, preferred_element_type=jnp.float32)
            total = lax.optimization_barrier(jnp.sum(expd, axis=1))
            weighted = lax.optimization_barrier(jnp.sum(expd * dprob, axis=1))
            prob = expd / total[:, None]
            dscore = prob * (dprob - (weighted / total)[:, None])
            prob_b = prob.astype(jnp.bfloat16)
            dscore_b = dscore.astype(jnp.bfloat16)
            dv_acc = dv_acc + jnp.dot(prob_b.T, d_one, preferred_element_type=jnp.float32)
            dk_acc = dk_acc + jnp.dot(dscore_b.T, q_one, preferred_element_type=jnp.float32)
            dq_one = jnp.dot(dscore_b, k_head, preferred_element_type=jnp.float32)
            return ((dk_acc, dv_acc), dq_one)
        start = (jnp.zeros((KEYS, HD), jnp.float32), jnp.zeros((KEYS, HD), jnp.float32))
        (dk_sum, dv_sum), dq_all = lax.scan(per_head, start, (q_heads, d_heads))
        return (dq_all, dk_sum, dv_sum)
    dq_g, dk_g, dv_g = lax.map(per_kv, (q_groups, d_groups, k_groups, v_groups))
    dqb = dq_g.transpose(2, 0, 1, 3).reshape(TXT, QH, HD)
    grad_q = dqb * HD ** (-0.5) * q_gain
    dq = rq * grad_q - q * rq ** 3 * lax.optimization_barrier(jnp.mean(q * grad_q, axis=-1, keepdims=True))
    dq_b = dq.reshape(TXT, QH * HD).astype(jnp.bfloat16)
    text_grad = jnp.dot(dq_b, w_query.T, preferred_element_type=jnp.float32)
    grad_k = dk_g.transpose(1, 0, 2) * k_gain
    key_grad = rk * grad_k - k * rk ** 3 * lax.optimization_barrier(jnp.mean(k * grad_k, axis=-1, keepdims=True))
    key_grad = key_grad.reshape(KEYS, KVH * HD)
    value_grad = dv_g.transpose(1, 0, 2).reshape(KEYS, KVH * HD)
    return (text_grad, key_grad, value_grad)
```

```python
import functools

import jax
import jax.numpy as jnp
from jax import lax
from jax.experimental import pallas as pl
from jax.experimental.pallas import tpu as pltpu
from jax.sharding import PartitionSpec as P

MESH = pl.DeviceIdType.MESH
BLK = 16
EPS = 1e-05
HD = 128
LAG = 2
SLOTS = LAG + 1
CHUNK = 320
F32 = jnp.float32
BF16 = jnp.bfloat16
NT = (((1,), (1,)), ((), ()))


def attention_kernel(
    heads, chips, rows, q_ref, qg_ref, k_ref, kg_ref, v_ref, d_ref, span_ref, len_ref,
    dq_ref, dk_ref, dv_ref,
    qd, e_buf, f_buf, kb, kt, km, rm, lu, lu_sib, lu_chip, lu_all, dq_part, dq_sib, dq_chip, dq_all,
    ag_send, ag_recv, fw_send, fw_recv, s1_send, s1_recv, s2_send, s2_recv,
    r1_send, r1_recv, r2_send, r2_recv,
):
    me = lax.axis_index("frame")
    core = lax.rem(me, 2)
    chip = me // 2
    sibling = me + 1 - 2 * core
    half = chips * rows
    every = 2 * half
    keys = k_ref.shape[0]
    peers = chips - 1

    def peer(k):
        return 2 * lax.rem(chip + k, chips) + core

    def push(src, dst, send, recv, target):
        return pltpu.make_async_remote_copy(
            src_ref=src, dst_ref=dst, send_sem=send, recv_sem=recv,
            device_id={"frame": target}, device_id_type=MESH,
        )

    barrier = pltpu.get_barrier_semaphore()
    pl.semaphore_signal(barrier, inc=1, device_id={"frame": sibling}, device_id_type=MESH)
    for k in range(1, chips):
        pl.semaphore_signal(barrier, inc=1, device_id={"frame": peer(k)}, device_id_type=MESH)

    mine = pl.multiple_of(core * half + chip * rows, rows)
    for h in range(heads):
        at = slice(h * HD, (h + 1) * HD)
        q = q_ref[:, at].astype(F32)
        scale = lax.rsqrt(jnp.mean(q * q, axis=-1, keepdims=True) + EPS)
        qd[h, pl.ds(mine, rows), :HD] = (q * scale * qg_ref[...] * HD ** (-0.5)).astype(BF16)
        qd[h, pl.ds(mine, rows), HD:] = d_ref[:, at]
    pl.semaphore_wait(barrier, chips)

    def gather_copy(h, k):
        block = qd.at[h, pl.ds(mine, rows)]
        return push(block, block, ag_send.at[h], ag_recv.at[h], peer(k))

    def gather_all(h):
        block = qd.at[h, pl.ds(0, peers * rows)]
        return push(block, block, ag_send.at[h], ag_recv.at[h], sibling)

    def forward(h):
        block = qd.at[h, pl.ds(pl.multiple_of(core * half, half), half)]
        return push(block, block, fw_send.at[h], fw_recv.at[h], sibling)

    def send_block(h, carry):
        for k in range(1, chips):
            gather_copy(h, k).start()
        return carry

    lax.fori_loop(0, heads, send_block, 0)

    k = k_ref[...].astype(F32)
    scale = lax.rsqrt(jnp.mean(k * k, axis=-1, keepdims=True) + EPS)
    k = k * scale * kg_ref[...]
    kb[...] = k.astype(BF16)
    kt[...] = k.T.astype(BF16)
    km[...] = (lax.broadcasted_iota(jnp.int32, km.shape, 0) < len_ref[0]).astype(F32)
    r = lax.broadcasted_iota(jnp.int32, (span_ref.shape[0], every), 1)
    owner = 2 * ((r % half) // rows) + r // half
    span_of = owner * (rows // BLK) + (r % rows) // BLK
    hit = span_of == lax.broadcasted_iota(jnp.int32, r.shape, 0)
    rm[...] = jnp.sum(jnp.where(hit & (span_ref[...] > 0), 1.0, 0.0), axis=0, keepdims=True)
    dk_ref[...] = jnp.zeros_like(dk_ref)
    dv_ref[...] = jnp.zeros_like(dv_ref)

    def stat_sib(h):
        return push(lu.at[h], lu_sib.at[h], s1_send.at[h], s1_recv.at[h], sibling)

    def stat_copy(h, k):
        return push(lu_chip.at[h], lu_all.at[h, chip], s2_send.at[h], s2_recv.at[h], peer(k))

    def stat_all(h):
        block = lu_all.at[h, pl.ds(0, peers)]
        return push(block, block, s2_send.at[h], s2_recv.at[h], sibling)

    def dq_to_sib(h):
        return push(
            dq_part.at[h, pl.ds(pl.multiple_of((1 - core) * half, half), half)], dq_sib.at[h],
            r1_send.at[h], r1_recv.at[h], sibling,
        )

    def dq_copy(h, k):
        to = lax.rem(chip + k, chips)
        return push(
            dq_chip.at[h, pl.ds(pl.multiple_of(to * rows, rows), rows)], dq_all.at[h, chip],
            r2_send.at[h], r2_recv.at[h], peer(k),
        )

    def dq_all_of(h):
        block = dq_all.at[h, pl.ds(0, peers)]
        return push(block, block, r2_send.at[h], r2_recv.at[h], sibling)

    def first_pass(h):
        slot = lax.rem(h, SLOTS)
        q, d = qd[h, :, :HD], qd[h, :, HD:]
        l = jnp.zeros((1, every), F32)
        u = jnp.zeros((1, every), F32)
        for m in range(0, keys, CHUNK):
            s = lax.dot_general(kb[m : m + CHUNK], q, NT, preferred_element_type=F32)
            dp = lax.dot_general(v_ref[m : m + CHUNK], d, NT, preferred_element_type=F32)
            live = jnp.concatenate([km[m : m + CHUNK]] * (every // HD), axis=1)
            e = jnp.exp(s) * live
            f = e * dp
            e_buf[slot, m : m + CHUNK] = e.astype(BF16)
            f_buf[slot, m : m + CHUNK] = f.astype(BF16)
            l += jnp.sum(e, axis=0, keepdims=True)
            u += jnp.sum(f, axis=0, keepdims=True)
        l *= rm[...]
        u *= rm[...]
        n = every // HD
        for i in range(n):
            lu[h, i : i + 1] = l[:, i * HD : (i + 1) * HD]
            lu[h, n + i : n + i + 1] = u[:, i * HD : (i + 1) * HD]

    def second_pass(h):
        slot = lax.rem(h, SLOTS)
        q, d = qd[h, :, :HD], qd[h, :, HD:]
        total = lu_all[h, 0]
        for c in range(1, chips):
            total = total + lu_all[h, c]
        n = every // HD
        l = jnp.concatenate([total[i : i + 1] for i in range(n)], axis=1)
        u = jnp.concatenate([total[n + i : n + i + 1] for i in range(n)], axis=1)
        il = rm[...] / l
        w = (u / l) * il
        col = jnp.concatenate([il] * 8, axis=0).T[:, 0:1]
        x = (d.astype(F32) * col).astype(BF16)
        for m in range(0, keys, CHUNK):
            e = e_buf[slot, m : m + CHUNK]
            f = f_buf[slot, m : m + CHUNK]
            ds = (f.astype(F32) * il - e.astype(F32) * w).astype(BF16)
            f_buf[slot, m : m + CHUNK] = ds
            dv_ref[m : m + CHUNK] += jnp.dot(e, x, preferred_element_type=F32)
            dk_ref[m : m + CHUNK] += jnp.dot(ds, q, preferred_element_type=F32)
        dqt = jnp.dot(kt[...], f_buf[slot], preferred_element_type=F32)
        dq_part[h] = dqt.T.astype(BF16)

    def second_dq(h):
        dq_to_sib(h).wait_recv()
        own = dq_part[h, pl.ds(pl.multiple_of(core * half, half), half)]
        dq_chip[h] = (own.astype(F32) + dq_sib[h].astype(F32)).astype(BF16)
        dq_all[h, chip] = dq_chip[h, pl.ds(pl.multiple_of(chip * rows, rows), rows)]
        for k in range(1, chips):
            dq_copy(h, k).start()

    gather_all(0).wait_recv()
    forward(0).start()

    def step(s, carry):
        @pl.when(s + 1 < heads)
        def _():
            gather_all(s + 1).wait_recv()
            forward(s + 1).start()

        @pl.when(s < heads)
        def _():
            forward(s).wait_recv()
            first_pass(s)
            stat_sib(s).start()

        @pl.when(s > LAG)
        def _():
            second_dq(s - LAG - 1)

        @pl.when(s >= LAG)
        def _():
            stat_all(s - LAG).wait_recv()
            second_pass(s - LAG)
            dq_to_sib(s - LAG).start()

        @pl.when(s < heads)
        def _():
            stat_sib(s).wait_recv()
            both = lu[s] + lu_sib[s]
            lu_chip[s] = both
            lu_all[s, chip] = both
            for k in range(1, chips):
                stat_copy(s, k).start()

        return carry

    lax.fori_loop(0, heads + LAG, step, 0)
    second_dq(heads - 1)

    def drain(h, carry):
        gather_all(h).wait_send()
        forward(h).wait_send()
        stat_sib(h).wait_send()
        stat_all(h).wait_send()
        dq_to_sib(h).wait_send()
        dq_all_of(h).wait_send()
        return carry

    for h in range(heads):
        dq_all_of(h).wait_recv()
        total = dq_all[h, 0].astype(F32)
        for c in range(1, chips):
            total = total + dq_all[h, c].astype(F32)
        at = slice(h * HD, (h + 1) * HD)
        q = q_ref[:, at].astype(F32)
        scale = lax.rsqrt(jnp.mean(q * q, axis=-1, keepdims=True) + EPS)
        g = total * HD ** (-0.5) * qg_ref[...]
        dq = scale * g - q * scale**3 * jnp.mean(q * g, axis=-1, keepdims=True)
        dq_ref[:, at] = dq.astype(BF16)
    lax.fori_loop(0, heads, drain, 0)


def attention(queries, q_gain, keys, k_gain, values, out_grad, span_col, frame_len):
    rows, width = queries.shape
    heads = width // HD
    chips = lax.axis_size("frame") // 2
    every = 2 * chips * rows
    n = keys.shape[0]
    vmem = pl.BlockSpec(memory_space=pltpu.VMEM)
    smem = pl.BlockSpec(memory_space=pltpu.SMEM)
    sems = pltpu.SemaphoreType.DMA((heads,))
    stat = 2 * every // HD
    return pl.pallas_call(
        functools.partial(attention_kernel, heads, chips, rows),
        out_shape=(
            jax.ShapeDtypeStruct((rows, width), BF16),
            jax.ShapeDtypeStruct((n, HD), F32),
            jax.ShapeDtypeStruct((n, HD), F32),
        ),
        in_specs=[vmem] * 7 + [smem],
        out_specs=(vmem, vmem, vmem),
        scratch_shapes=[
            pltpu.VMEM((heads, every, 2 * HD), BF16),
            pltpu.VMEM((SLOTS, n, every), BF16),
            pltpu.VMEM((SLOTS, n, every), BF16),
            pltpu.VMEM((n, HD), BF16),
            pltpu.VMEM((HD, n), BF16),
            pltpu.VMEM((n, HD), F32),
            pltpu.VMEM((1, every), F32),
            pltpu.VMEM((heads, stat, HD), F32),
            pltpu.VMEM((heads, stat, HD), F32),
            pltpu.VMEM((heads, stat, HD), F32),
            pltpu.VMEM((heads, chips, stat, HD), F32),
            pltpu.VMEM((heads, every, HD), BF16),
            pltpu.VMEM((heads, every // 2, HD), BF16),
            pltpu.VMEM((heads, every // 2, HD), BF16),
            pltpu.VMEM((heads, chips, rows, HD), BF16),
        ] + [sems] * 12,
        compiler_params=pltpu.CompilerParams(
            collective_id=0, has_side_effects=True, vmem_limit_bytes=56 * 2**20
        ),
        cost_estimate=pl.CostEstimate(
            flops=10 * heads * every * n * HD, bytes_accessed=2**23, transcendentals=heads * every * n
        ),
    )(queries, q_gain[None], keys, k_gain[None], values, out_grad, span_col, frame_len)


def summed_on_arrival(value, axis, dim):
    before, after = value.shape[:dim], value.shape[dim + 1 :]
    parts = jnp.moveaxis(value.reshape(*before, lax.axis_size(axis), -1, *after), dim, 0)
    arrived = lax.all_to_all(parts, axis, split_axis=0, concat_axis=0, tiled=True)
    return arrived.astype(F32).sum(axis=0)


def local(queries, q_gain, keys, k_gain, values, out_grad, w_query, span_mask, frame_len):
    dq_raw, dk_acc, dv_acc = attention(
        queries, q_gain, keys, k_gain, values, out_grad, span_mask, frame_len
    )
    text_term = lax.dot_general(dq_raw, w_query, (((1,), (1,)), ((), ())), preferred_element_type=F32)
    text_grad = summed_on_arrival(text_term.astype(BF16), "head", 1)
    k_raw = keys.astype(F32)
    k_scale = lax.rsqrt(jnp.mean(k_raw * k_raw, axis=-1, keepdims=True) + EPS)
    g = dk_acc * k_gain
    key_grad = k_scale * g - k_raw * k_scale**3 * jnp.mean(k_raw * g, axis=-1, keepdims=True)
    return (text_grad, key_grad, dv_acc)


def solution(mesh):
    return jax.shard_map(
        local,
        mesh=mesh,
        in_specs=(
            P("frame", "head"), P(), P("frame", "head"), P(), P("frame", "head"),
            P("frame", "head"), P(None, "head"), P(None, "frame"), P("frame"),
        ),
        out_specs=(P("frame", "head"), P("frame", "head"), P("frame", "head")),
        check_vma=False,
    )
```

```python
import functools

import jax
import jax.numpy as jnp
from jax import lax
from jax.experimental import pallas as pl
from jax.experimental.pallas import tpu as pltpu
from jax.sharding import PartitionSpec as P

MESH = pl.DeviceIdType.MESH
BLK = 16
EPS = 1e-05
HD = 128
LAG = 2
SLOTS = LAG + 1
CHUNK = 320
F32 = jnp.float32
BF16 = jnp.bfloat16
NT = (((1,), (1,)), ((), ()))


def kernel(
    heads, rows, q_ref, qg_ref, k_ref, kg_ref, v_ref, d_ref, span_ref, len_ref, w_ref,
    text_ref, dk_ref, dv_ref,
    qd, e_buf, f_buf, kb, kt, km, rm, dk, dv, lu, lu_in, lu_chip, lu_all, dq_part, dq_in0, dq_s0, dq_in1, dq_s1,
    dq_in2, dq, w_buf, t_out, t_in,
    ag_send, ag_recv, st_send, st_recv, rs_send, rs_recv, tx_send, tx_recv, w_sem, out_sem,
):
    frame = lax.axis_index("frame")
    head = lax.axis_index("head")
    core = lax.rem(frame, 2)
    z = lax.rem(frame // 2, 4)
    x = frame // 8
    chip = frame // 2
    half = 8 * rows
    every = 2 * half
    keys = k_ref.shape[0]
    groups = every // HD
    cols = text_ref.shape[1]

    def frame_of(x_, z_, core_):
        return {"frame": x_ * 8 + z_ * 2 + core_}

    def around(k):
        return lax.rem(z + k, 4)

    sib = frame_of(x, z, 1 - core)
    x_near = frame_of(1 - x, z, core)

    def peer(k):
        return {"frame": 2 * lax.rem(chip + k, 8) + core}

    def group(k):
        return lax.rem(head + k, 8)

    def push(src, dst, send, recv, target):
        return pltpu.make_async_remote_copy(
            src_ref=src, dst_ref=dst, send_sem=send, recv_sem=recv, device_id=target, device_id_type=MESH
        )

    def span_of_rows(first, count, size):
        return pl.ds(pl.multiple_of(first, size), count)

    barrier = pltpu.get_barrier_semaphore()
    pl.semaphore_signal(barrier, inc=1, device_id=sib, device_id_type=MESH)
    for k in range(1, 8):
        pl.semaphore_signal(barrier, inc=1, device_id=peer(k), device_id_type=MESH)
        pl.semaphore_signal(barrier, inc=1, device_id={"head": group(k)}, device_id_type=MESH)

    def index(par, x_, z_):
        return x_ * 4 + z_ if par == 0 else z_ * 2 + x_

    def gather(h, par, stage):
        if stage == 2:
            block = qd.at[h, span_of_rows(core * half, half, half)]
            return [push(block, block, ag_send.at[2, h], ag_recv.at[2, h], sib)]
        if par == 0:
            first, blocks = ((index(0, x, z), 1), (x * 4, 4))[stage]
            along_z = stage == 0
        else:
            first, blocks = ((index(1, x, z), 1), (z * 2, 2))[stage]
            along_z = stage == 1
        block = qd.at[h, span_of_rows(core * half + first * rows, blocks * rows, rows)]
        targets = [frame_of(x, around(k), core) for k in (1, 2, 3)] if along_z else [x_near]
        return [push(block, block, ag_send.at[stage, h], ag_recv.at[stage, h], t) for t in targets]

    def gather_bytes(h, par, stage):
        count = (half, (3 * rows, 4 * rows), (rows, 6 * rows))[0 if stage == 2 else 1 + par]
        count = count if stage == 2 else count[stage]
        block = qd.at[h, pl.ds(0, count)]
        return push(block, block, ag_send.at[stage, h], ag_recv.at[stage, h], sib)

    def go(copies):
        for copy in copies:
            copy.start()

    def advance(h, par, stage):
        gather_bytes(h, par, stage).wait_recv()
        go(gather(h, par, stage + 1))

    def head_rows(h):
        at = slice(h * HD, (h + 1) * HD)
        mine = span_of_rows(core * half + index(h % 2, x, z) * rows, rows, rows)
        q = q_ref[:, at].astype(F32)
        scale = lax.rsqrt(jnp.mean(q * q, axis=-1, keepdims=True) + EPS)
        qd[h, mine, :HD] = (q * scale * qg_ref[...] * HD ** (-0.5)).astype(BF16)
        qd[h, mine, HD:] = d_ref[:, at]

    def first_block(k):
        block = qd.at[0, span_of_rows(core * half + index(0, x, z) * rows, rows, rows)]
        return push(block, block, ag_send.at[0, 0], ag_recv.at[0, 0], peer(k))

    def first_bytes():
        block = qd.at[0, pl.ds(0, 7 * rows)]
        return push(block, block, ag_send.at[0, 0], ag_recv.at[0, 0], sib)

    head_rows(0)
    pl.semaphore_wait(barrier, 15)
    for k in range(1, 8):
        first_block(k).start()
    head_rows(1)
    go(gather(1, 1, 0))
    for h in range(2, heads):
        head_rows(h)
    for t in range(heads):
        pltpu.make_async_copy(w_ref.at[pl.ds(t * cols, cols)], w_buf.at[t], w_sem.at[t]).start()

    k = k_ref[...].astype(F32)
    k_scale = lax.rsqrt(jnp.mean(k * k, axis=-1, keepdims=True) + EPS)
    k = k * k_scale * kg_ref[...]
    kb[...] = k.astype(BF16)
    kt[...] = k.T.astype(BF16)
    advance(1, 1, 0)
    go(gather(2, 0, 0))
    km[...] = (lax.broadcasted_iota(jnp.int32, km.shape, 0) < len_ref[0]).astype(F32)
    spans = span_ref.shape[1]
    r = lax.broadcasted_iota(jnp.int32, (spans, every), 1)
    i = (r // rows) % 8
    for par in range(2):
        chip_of = i if par == 0 else (i % 2) * 4 + i // 2
        span_of = (chip_of * 2 + r // half) * (rows // BLK) + (r % rows) // BLK
        hit = (span_of == lax.broadcasted_iota(jnp.int32, r.shape, 0)).astype(F32)
        seen = jnp.broadcast_to((span_ref[...] > 0).astype(F32), (8, spans))
        rm[par] = jnp.dot(seen, hit, preferred_element_type=F32)[0:1]
    dk[...] = jnp.zeros_like(dk)
    dv[...] = jnp.zeros_like(dv)
    first_bytes().wait_recv()
    go(gather(0, 0, 2))

    def stat(h):
        return push(lu.at[h], lu_in.at[h], st_send.at[0, h], st_recv.at[0, h], sib)

    def stat_out(h, k):
        return push(lu_chip.at[h], lu_all.at[h, chip], st_send.at[1, h], st_recv.at[1, h], peer(k))

    def stat_bytes(h):
        block = lu_all.at[h, pl.ds(0, 7)]
        return push(block, block, st_send.at[1, h], st_recv.at[1, h], sib)

    def stat_spread(h):
        stat(h).wait_recv()
        both = lu[h] + lu_in[h]
        lu_chip[h] = both
        lu_all[h, chip] = both
        for k in range(1, 8):
            stat_out(h, k).start()

    def reduce_sib(h):
        src = dq_part.at[h, span_of_rows((1 - core) * half, half, half)]
        return push(src, dq_in0.at[h], rs_send.at[0, h], rs_recv.at[0, h], sib)

    def reduce(h, par, stage):
        if par == 0 and stage == 1:
            src = dq_s0.at[h, span_of_rows((1 - x) * 4 * rows, 4 * rows, 4 * rows)]
            return [push(src, dq_in1.at[h, pl.ds(0, 4 * rows)], rs_send.at[1, h], rs_recv.at[1, h], x_near)]
        if par == 1 and stage == 2:
            src = dq_s1.at[h, span_of_rows((1 - x) * rows, rows, rows)]
            return [push(src, dq_in2.at[h, pl.ds(0, rows)], rs_send.at[2, h], rs_recv.at[2, h], x_near)]
        copies = []
        for k in (1, 2, 3):
            to = around(k)
            if par == 0:
                src = dq_s1.at[h, span_of_rows(to * rows, rows, rows)]
                dst = dq_in2.at[h, pl.ds((3 - k) * rows, rows)]
            else:
                src = dq_s0.at[h, span_of_rows(to * 2 * rows, 2 * rows, 2 * rows)]
                dst = dq_in1.at[h, pl.ds((3 - k) * 2 * rows, 2 * rows)]
            copies.append(push(src, dst, rs_send.at[stage, h], rs_recv.at[stage, h], frame_of(x, to, core)))
        return copies

    def reduce_bytes(h, par, stage):
        count = ((4, 3), (6, 1))[par][stage - 1] * rows
        block = (dq_in1 if stage == 1 else dq_in2).at[h, pl.ds(0, count)]
        return push(block, block, rs_send.at[stage, h], rs_recv.at[stage, h], sib)

    def reduce_first(h, par):
        reduce_sib(h).wait_recv()
        own = dq_part[h, span_of_rows(core * half, half, half)]
        dq_s0[h] = (own.astype(F32) + dq_in0[h].astype(F32)).astype(BF16)
        go(reduce(h, par, 1))

    def reduce_second(h, par):
        reduce_bytes(h, par, 1).wait_recv()
        if par == 0:
            own = dq_s0[h, span_of_rows(x * 4 * rows, 4 * rows, 4 * rows)].astype(F32)
            dq_s1[h] = (own + dq_in1[h, : 4 * rows].astype(F32)).astype(BF16)
        else:
            total = dq_s0[h, span_of_rows(z * 2 * rows, 2 * rows, 2 * rows)].astype(F32)
            for k in range(3):
                total = total + dq_in1[h, k * 2 * rows : (k + 1) * 2 * rows].astype(F32)
            dq_s1[h, : 2 * rows] = total.astype(BF16)
        go(reduce(h, par, 2))

    def finish(h):
        par = h % 2
        reduce_bytes(h, par, 2).wait_recv()
        mine = z if par == 0 else x
        total = dq_s1[h, span_of_rows(mine * rows, rows, rows)].astype(F32)
        for k in range(3 if par == 0 else 1):
            total = total + dq_in2[h, k * rows : (k + 1) * rows].astype(F32)
        at = slice(h * HD, (h + 1) * HD)
        q = q_ref[:, at].astype(F32)
        scale = lax.rsqrt(jnp.mean(q * q, axis=-1, keepdims=True) + EPS)
        g = total * HD ** (-0.5) * qg_ref[...]
        g = scale * g - q * scale**3 * jnp.mean(q * g, axis=-1, keepdims=True)
        dq[:, at] = g.astype(BF16)

    def first_pass(h, par):
        slot = lax.rem(h, SLOTS)
        q, d = qd[h, :, :HD], qd[h, :, HD:]
        l = jnp.zeros((1, every), F32)
        u = jnp.zeros((1, every), F32)
        for m in range(0, keys, CHUNK):
            s = lax.dot_general(kb[m : m + CHUNK], q, NT, preferred_element_type=F32)
            dp = lax.dot_general(v_ref[m : m + CHUNK], d, NT, preferred_element_type=F32)
            live = jnp.concatenate([km[m : m + CHUNK]] * groups, axis=1)
            e = jnp.exp(s) * live
            f = e * dp
            e_buf[slot, m : m + CHUNK] = e.astype(BF16)
            f_buf[slot, m : m + CHUNK] = f.astype(BF16)
            l += jnp.sum(e, axis=0, keepdims=True)
            u += jnp.sum(f, axis=0, keepdims=True)
        l *= rm[par]
        u *= rm[par]
        for j in range(groups):
            lu[h, j : j + 1] = l[:, j * HD : (j + 1) * HD]
            lu[h, groups + j : groups + j + 1] = u[:, j * HD : (j + 1) * HD]

    def row_factors(h, par):
        total = lu_all[h, 0]
        for c in range(1, 8):
            total = total + lu_all[h, c]
        l = jnp.concatenate([total[j : j + 1] for j in range(groups)], axis=1)
        u = jnp.concatenate([total[groups + j : groups + j + 1] for j in range(groups)], axis=1)
        il = rm[par] / l
        return il, (u / l) * il

    def query_grads(h, par):
        slot = lax.rem(h, SLOTS)
        il, w = row_factors(h, par)
        for m in range(0, keys, CHUNK):
            e = e_buf[slot, m : m + CHUNK].astype(F32)
            f = f_buf[slot, m : m + CHUNK].astype(F32)
            f_buf[slot, m : m + CHUNK] = (f * il - e * w).astype(BF16)
        dq_part[h] = jnp.dot(kt[...], f_buf[slot], preferred_element_type=F32).T.astype(BF16)

    def frame_grads(h, par):
        slot = lax.rem(h, SLOTS)
        il, _ = row_factors(h, par)
        col = jnp.concatenate([il] * 8, axis=0).T[:, 0:1]
        d = (qd[h, :, HD:].astype(F32) * col).astype(BF16)
        q = qd[h, :, :HD]
        for m in range(0, keys, CHUNK):
            dv[m : m + CHUNK] += jnp.dot(e_buf[slot, m : m + CHUNK], d, preferred_element_type=F32)
            dk[m : m + CHUNK] += jnp.dot(f_buf[slot, m : m + CHUNK], q, preferred_element_type=F32)

    def step(s, par):
        odd = 1 - par

        @pl.when(s < heads)
        def _():
            gather_bytes(s, par, 2).wait_recv()
            first_pass(s, par)
            stat(s).start()

        @pl.when(s + 1 < heads)
        def _():
            advance(s + 1, odd, 1)

        @pl.when(s + 2 < heads)
        def _():
            advance(s + 2, par, 0)

        @pl.when(s + 3 < heads)
        def _():
            go(gather(s + 3, odd, 0))

        @pl.when(s >= LAG)
        def _():
            stat_bytes(s - LAG).wait_recv()
            query_grads(s - LAG, par)
            reduce_sib(s - LAG).start()

        @pl.when(s < heads)
        def _():
            stat_spread(s)

        @pl.when(s >= LAG)
        def _():
            frame_grads(s - LAG, par)
            reduce_first(s - LAG, par)

        @pl.when(s > LAG)
        def _():
            reduce_second(s - LAG - 1, odd)

    def pair(t, carry):
        step(2 * t, 0)
        step(2 * t + 1, 1)
        return carry

    lax.fori_loop(0, (heads + LAG) // 2, pair, 0)

    for h in range(heads - 2):
        finish(h)
    for t in range(heads):
        pltpu.make_async_copy(w_ref.at[pl.ds(t * cols, cols)], w_buf.at[t], w_sem.at[t]).wait()
    dv_out = pltpu.make_async_copy(dv, dv_ref, out_sem.at[0])
    dv_out.start()
    reduce_second(heads - 1, (heads - 1) % 2)
    k = k_ref[...].astype(F32)
    k_scale = lax.rsqrt(jnp.mean(k * k, axis=-1, keepdims=True) + EPS)
    g = dk[...] * kg_ref[...]
    dk[...] = k_scale * g - k * k_scale**3 * jnp.mean(k * g, axis=-1, keepdims=True)
    dk_out = pltpu.make_async_copy(dk, dk_ref, out_sem.at[1])
    dk_out.start()
    finish(heads - 2)
    finish(heads - 1)

    def text(k):
        return push(t_out.at[k], t_in.at[7 - k], tx_send.at[k], tx_recv.at[7 - k], {"head": group(k)})

    def term(to):
        return lax.dot_general(dq[...], w_buf[to], NT, preferred_element_type=F32)

    for k in (3, 5, 4, 1, 7, 2, 6):
        t_out[k] = term(group(k)).astype(BF16)
        text(k).start()
    total = term(head)

    def drain(h, carry):
        stat(h).wait_send()
        stat_bytes(h).wait_send()
        reduce_sib(h).wait_send()
        gather_bytes(h, 0, 2).wait_send()
        return carry

    def drain_pair(t, carry):
        for par in range(2):
            h = 2 * t + par
            reduce_bytes(h, par, 1).wait_send()
            reduce_bytes(h, par, 2).wait_send()

            @pl.when(h > 0)
            def _():
                gather_bytes(h, par, 0).wait_send()
                gather_bytes(h, par, 1).wait_send()

        return carry

    lax.fori_loop(0, heads, drain, 0)
    lax.fori_loop(0, heads // 2, drain_pair, 0)
    first_bytes().wait_send()
    for k in (4, 2, 3, 6, 0, 5, 1):
        text(7 - k).wait_recv()
        total = total + t_in[k].astype(F32)
    text_ref[...] = total
    for k in range(1, 8):
        text(k).wait_send()
    dv_out.wait()
    dk_out.wait()


def copy_kernel(*refs):
    for src, dst in zip(refs[:3], refs[3:]):
        dst[...] = src[...]


def local(queries, q_gain, keys, k_gain, values, out_grad, w_query, span_mask, frame_len):
    rows, width = queries.shape
    heads = width // HD
    every = lax.axis_size("frame") * rows
    half = every // 2
    n = keys.shape[0]
    cols = w_query.shape[0] // lax.axis_size("head")
    vmem = pl.BlockSpec(memory_space=pltpu.VMEM)
    smem = pl.BlockSpec(memory_space=pltpu.SMEM)
    anywhere = pl.BlockSpec(memory_space=pl.ANY)
    stat = 2 * every // HD
    sems = pltpu.SemaphoreType.DMA
    results = pl.pallas_call(
        functools.partial(kernel, heads, rows),
        out_shape=(
            jax.ShapeDtypeStruct((rows, cols), F32),
            jax.ShapeDtypeStruct((n, HD), F32),
            jax.ShapeDtypeStruct((n, HD), F32),
        ),
        in_specs=[vmem] * 7 + [smem, anywhere],
        out_specs=(vmem, anywhere, anywhere),
        scratch_shapes=[
            pltpu.VMEM((heads, every, 2 * HD), BF16),
            pltpu.VMEM((SLOTS, n, every), BF16),
            pltpu.VMEM((SLOTS, n, every), BF16),
            pltpu.VMEM((n, HD), BF16),
            pltpu.VMEM((HD, n), BF16),
            pltpu.VMEM((n, HD), F32),
            pltpu.VMEM((2, 1, every), F32),
            pltpu.VMEM((n, HD), F32),
            pltpu.VMEM((n, HD), F32),
            pltpu.VMEM((heads, stat, HD), F32),
            pltpu.VMEM((heads, stat, HD), F32),
            pltpu.VMEM((heads, stat, HD), F32),
            pltpu.VMEM((heads, 8, stat, HD), F32),
            pltpu.VMEM((heads, every, HD), BF16),
            pltpu.VMEM((heads, half, HD), BF16),
            pltpu.VMEM((heads, half, HD), BF16),
            pltpu.VMEM((heads, 6 * rows, HD), BF16),
            pltpu.VMEM((heads, 4 * rows, HD), BF16),
            pltpu.VMEM((heads, 3 * rows, HD), BF16),
            pltpu.VMEM((rows, width), BF16),
            pltpu.VMEM((heads, cols, width), BF16),
            pltpu.VMEM((8, rows, cols), BF16),
            pltpu.VMEM((8, rows, cols), BF16),
        ]
        + [sems((3, heads))] * 2
        + [sems((2, heads))] * 2
        + [sems((3, heads))] * 2
        + [sems((8,))] * 2
        + [sems((heads,)), sems((2,))],
        compiler_params=pltpu.CompilerParams(
            collective_id=0, has_side_effects=True, vmem_limit_bytes=62 * 2**20
        ),
        cost_estimate=pl.CostEstimate(
            flops=10 * heads * every * n * HD, bytes_accessed=2**25, transcendentals=heads * every * n
        ),
    )(
        queries, q_gain[None], keys, k_gain[None], values, out_grad, span_mask.reshape(1, -1), frame_len, w_query
    )
    return pl.pallas_call(
        copy_kernel,
        out_shape=[jax.ShapeDtypeStruct(a.shape, a.dtype) for a in results],
        in_specs=[vmem] * 3,
        out_specs=[vmem] * 3,
    )(*results)


def solution(mesh):
    return jax.shard_map(
        local,
        mesh=mesh,
        in_specs=(
            P("frame", "head"), P(), P("frame", "head"), P(), P("frame", "head"),
            P("frame", "head"), P(None, "head"), P(None, "frame"), P("frame"),
        ),
        out_specs=(P("frame", "head"), P("frame", "head"), P("frame", "head")),
        check_vma=False,
    )
```

```python
import functools

import jax
import jax.numpy as jnp
from jax import lax
from jax.experimental import pallas as pl
from jax.experimental.pallas import tpu as pltpu
from jax.sharding import PartitionSpec as P

MESH = pl.DeviceIdType.MESH
BLK = 16
EPS = 1e-05
HD = 128
LAG = 2
SLOTS = LAG + 1
CHUNK = 320
DIRECT = 4
F32 = jnp.float32
BF16 = jnp.bfloat16
NT = (((1,), (1,)), ((), ()))


def kernel(
    heads, rows, q_ref, qg_ref, k_ref, kg_ref, v_ref, d_ref, span_ref, len_ref, w_ref,
    text_ref, dk_ref, dv_ref,
    qd, e_buf, f_buf, kb, kt, km, rm, dk, dv, lu, lu_in, lu_chip, lu_all, dq_part, dq_in0, dq_s0, dq_in1, dq_s1,
    dq_in2, dq_last, dq, w_buf, t_sum, t_out, t_in,
    ag_send, ag_recv, st_send, st_recv, rs_send, rs_recv, tx_send, tx_recv, w_sem, out_sem,
):
    frame = lax.axis_index("frame")
    head = lax.axis_index("head")
    core = lax.rem(frame, 2)
    z = lax.rem(frame // 2, 4)
    x = frame // 8
    chip = frame // 2
    half = 8 * rows
    every = 2 * half
    keys = k_ref.shape[0]
    groups = every // HD
    cols = text_ref.shape[1]

    def frame_of(x_, z_, core_):
        return {"frame": x_ * 8 + z_ * 2 + core_}

    def around(k):
        return lax.rem(z + k, 4)

    sib = frame_of(x, z, 1 - core)
    x_near = frame_of(1 - x, z, core)

    def peer(k):
        return {"frame": 2 * lax.rem(chip + k, 8) + core}

    def group(k):
        return lax.rem(head + k, 8)

    def push(src, dst, send, recv, target):
        return pltpu.make_async_remote_copy(
            src_ref=src, dst_ref=dst, send_sem=send, recv_sem=recv, device_id=target, device_id_type=MESH
        )

    def span_of_rows(first, count, size):
        return pl.ds(pl.multiple_of(first, size), count)

    barrier = pltpu.get_barrier_semaphore()
    pl.semaphore_signal(barrier, inc=1, device_id=sib, device_id_type=MESH)
    for k in range(1, 8):
        pl.semaphore_signal(barrier, inc=1, device_id=peer(k), device_id_type=MESH)
        pl.semaphore_signal(barrier, inc=1, device_id={"head": group(k)}, device_id_type=MESH)

    def index(par, x_, z_):
        return x_ * 4 + z_ if par == 0 else z_ * 2 + x_

    def gather(h, par, stage):
        if stage == 2:
            block = qd.at[h, span_of_rows(core * half, half, half)]
            return [push(block, block, ag_send.at[2, h], ag_recv.at[2, h], sib)]
        if par == 0:
            first, blocks = ((index(0, x, z), 1), (x * 4, 4))[stage]
            along_z = stage == 0
        else:
            first, blocks = ((index(1, x, z), 1), (z * 2, 2))[stage]
            along_z = stage == 1
        block = qd.at[h, span_of_rows(core * half + first * rows, blocks * rows, rows)]
        targets = [frame_of(x, around(k), core) for k in (1, 2, 3)] if along_z else [x_near]
        return [push(block, block, ag_send.at[stage, h], ag_recv.at[stage, h], t) for t in targets]

    def gather_bytes(h, par, stage):
        count = (half, (3 * rows, 4 * rows), (rows, 6 * rows))[0 if stage == 2 else 1 + par]
        count = count if stage == 2 else count[stage]
        block = qd.at[h, pl.ds(0, count)]
        return push(block, block, ag_send.at[stage, h], ag_recv.at[stage, h], sib)

    def go(copies):
        for copy in copies:
            copy.start()

    def advance(h, par, stage):
        gather_bytes(h, par, stage).wait_recv()
        go(gather(h, par, stage + 1))

    def head_rows(h):
        at = slice(h * HD, (h + 1) * HD)
        mine = span_of_rows(core * half + index(h % 2, x, z) * rows, rows, rows)
        q = q_ref[:, at].astype(F32)
        scale = lax.rsqrt(jnp.mean(q * q, axis=-1, keepdims=True) + EPS)
        qd[h, mine, :HD] = (q * scale * qg_ref[...] * HD ** (-0.5)).astype(BF16)
        qd[h, mine, HD:] = d_ref[:, at]

    def direct(h, par, k):
        block = qd.at[h, span_of_rows(core * half + index(par, x, z) * rows, rows, rows)]
        return push(block, block, ag_send.at[0, h], ag_recv.at[0, h], peer(k))

    def direct_bytes(h):
        block = qd.at[h, pl.ds(0, 7 * rows)]
        return push(block, block, ag_send.at[0, h], ag_recv.at[0, h], sib)

    head_rows(0)
    pl.semaphore_wait(barrier, 15)
    for h in range(heads):
        if h > 0:
            head_rows(h)
        if h < DIRECT:
            for k in range(1, 8):
                direct(h, h % 2, k).start()
    for t in range(heads):
        pltpu.make_async_copy(w_ref.at[pl.ds(t * cols, cols)], w_buf.at[t], w_sem.at[t]).start()

    k = k_ref[...].astype(F32)
    k_scale = lax.rsqrt(jnp.mean(k * k, axis=-1, keepdims=True) + EPS)
    k = k * k_scale * kg_ref[...]
    kb[...] = k.astype(BF16)
    kt[...] = k.T.astype(BF16)
    km[...] = (lax.broadcasted_iota(jnp.int32, km.shape, 0) < len_ref[0]).astype(F32)
    spans = span_ref.shape[1]
    r = lax.broadcasted_iota(jnp.int32, (spans, every), 1)
    i = (r // rows) % 8
    for par in range(2):
        chip_of = i if par == 0 else (i % 2) * 4 + i // 2
        span_of = (chip_of * 2 + r // half) * (rows // BLK) + (r % rows) // BLK
        hit = (span_of == lax.broadcasted_iota(jnp.int32, r.shape, 0)).astype(F32)
        seen = jnp.broadcast_to((span_ref[...] > 0).astype(F32), (8, spans))
        rm[par] = jnp.dot(seen, hit, preferred_element_type=F32)[0:1]
    dk[...] = jnp.zeros_like(dk)
    dv[...] = jnp.zeros_like(dv)
    direct_bytes(0).wait_recv()
    go(gather(0, 0, 2))

    def stat(h):
        return push(lu.at[h], lu_in.at[h], st_send.at[0, h], st_recv.at[0, h], sib)

    def stat_out(h, k):
        return push(lu_chip.at[h], lu_all.at[h, chip], st_send.at[1, h], st_recv.at[1, h], peer(k))

    def stat_bytes(h):
        block = lu_all.at[h, pl.ds(0, 7)]
        return push(block, block, st_send.at[1, h], st_recv.at[1, h], sib)

    def stat_spread(h):
        stat(h).wait_recv()
        both = lu[h] + lu_in[h]
        lu_chip[h] = both
        lu_all[h, chip] = both
        for k in range(1, 8):
            stat_out(h, k).start()

    def reduce_sib(h):
        src = dq_part.at[h, span_of_rows((1 - core) * half, half, half)]
        return push(src, dq_in0.at[h], rs_send.at[0, h], rs_recv.at[0, h], sib)

    def reduce(h, par, stage):
        if par == 0 and stage == 1:
            src = dq_s0.at[h, span_of_rows((1 - x) * 4 * rows, 4 * rows, 4 * rows)]
            return [push(src, dq_in1.at[h, pl.ds(0, 4 * rows)], rs_send.at[1, h], rs_recv.at[1, h], x_near)]
        if par == 1 and stage == 2:
            src = dq_s1.at[h, span_of_rows((1 - x) * rows, rows, rows)]
            return [push(src, dq_in2.at[h, pl.ds(0, rows)], rs_send.at[2, h], rs_recv.at[2, h], x_near)]
        copies = []
        for k in (1, 2, 3):
            to = around(k)
            if par == 0:
                src = dq_s1.at[h, span_of_rows(to * rows, rows, rows)]
                dst = dq_in2.at[h, pl.ds((3 - k) * rows, rows)]
            else:
                src = dq_s0.at[h, span_of_rows(to * 2 * rows, 2 * rows, 2 * rows)]
                dst = dq_in1.at[h, pl.ds((3 - k) * 2 * rows, 2 * rows)]
            copies.append(push(src, dst, rs_send.at[stage, h], rs_recv.at[stage, h], frame_of(x, to, core)))
        return copies

    def reduce_bytes(h, par, stage):
        count = ((4, 3), (6, 1))[par][stage - 1] * rows
        block = (dq_in1 if stage == 1 else dq_in2).at[h, pl.ds(0, count)]
        return push(block, block, rs_send.at[stage, h], rs_recv.at[stage, h], sib)

    def last(k):
        to = lax.rem(chip + k, 8)
        src = dq_s0.at[heads - 1, span_of_rows(index(1, to // 4, lax.rem(to, 4)) * rows, rows, rows)]
        return push(src, dq_last.at[7 - k], rs_send.at[1, heads - 1], rs_recv.at[1, heads - 1], peer(k))

    def last_bytes():
        block = dq_last.at[pl.ds(0, 7)]
        return push(block, block, rs_send.at[1, heads - 1], rs_recv.at[1, heads - 1], sib)

    def reduce_first(h, par):
        reduce_sib(h).wait_recv()
        own = dq_part[h, span_of_rows(core * half, half, half)]
        dq_s0[h] = (own.astype(F32) + dq_in0[h].astype(F32)).astype(BF16)

        @pl.when(h < heads - 1)
        def _():
            go(reduce(h, par, 1))

        if par == 1:

            @pl.when(h == heads - 1)
            def _():
                for k in range(1, 8):
                    last(k).start()

    def reduce_second(h, par):
        reduce_bytes(h, par, 1).wait_recv()
        if par == 0:
            own = dq_s0[h, span_of_rows(x * 4 * rows, 4 * rows, 4 * rows)].astype(F32)
            dq_s1[h] = (own + dq_in1[h, : 4 * rows].astype(F32)).astype(BF16)
        else:
            total = dq_s0[h, span_of_rows(z * 2 * rows, 2 * rows, 2 * rows)].astype(F32)
            for k in range(3):
                total = total + dq_in1[h, k * 2 * rows : (k + 1) * 2 * rows].astype(F32)
            dq_s1[h, : 2 * rows] = total.astype(BF16)
        go(reduce(h, par, 2))

    def finish(h):
        par = h % 2
        if h == heads - 1:
            last_bytes().wait_recv()
            total = dq_s0[h, span_of_rows(index(1, x, z) * rows, rows, rows)].astype(F32)
            for k in range(7):
                total = total + dq_last[k].astype(F32)
        else:
            reduce_bytes(h, par, 2).wait_recv()
            mine = z if par == 0 else x
            total = dq_s1[h, span_of_rows(mine * rows, rows, rows)].astype(F32)
            for k in range(3 if par == 0 else 1):
                total = total + dq_in2[h, k * rows : (k + 1) * rows].astype(F32)
        at = slice(h * HD, (h + 1) * HD)
        q = q_ref[:, at].astype(F32)
        scale = lax.rsqrt(jnp.mean(q * q, axis=-1, keepdims=True) + EPS)
        g = total * HD ** (-0.5) * qg_ref[...]
        g = scale * g - q * scale**3 * jnp.mean(q * g, axis=-1, keepdims=True)
        dq[:, at] = g.astype(BF16)

    def first_pass(h, par, between):
        slot = lax.rem(h, SLOTS)
        q, d = qd[h, :, :HD], qd[h, :, HD:]
        l = jnp.zeros((1, every), F32)
        u = jnp.zeros((1, every), F32)
        for m in range(0, keys, CHUNK):
            s = lax.dot_general(kb[m : m + CHUNK], q, NT, preferred_element_type=F32)
            dp = lax.dot_general(v_ref[m : m + CHUNK], d, NT, preferred_element_type=F32)
            live = jnp.concatenate([km[m : m + CHUNK]] * groups, axis=1)
            e = jnp.exp(s) * live
            f = e * dp
            e_buf[slot, m : m + CHUNK] = e.astype(BF16)
            f_buf[slot, m : m + CHUNK] = f.astype(BF16)
            l += jnp.sum(e, axis=0, keepdims=True)
            u += jnp.sum(f, axis=0, keepdims=True)
            if m == 2 * CHUNK:
                between()
        l *= rm[par]
        u *= rm[par]
        for j in range(groups):
            lu[h, j : j + 1] = l[:, j * HD : (j + 1) * HD]
            lu[h, groups + j : groups + j + 1] = u[:, j * HD : (j + 1) * HD]

    def row_factors(h, par):
        total = lu_all[h, 0]
        for c in range(1, 8):
            total = total + lu_all[h, c]
        l = jnp.concatenate([total[j : j + 1] for j in range(groups)], axis=1)
        u = jnp.concatenate([total[groups + j : groups + j + 1] for j in range(groups)], axis=1)
        il = rm[par] / l
        return il, (u / l) * il

    def score_grads(h, par):
        slot = lax.rem(h, SLOTS)
        il, w = row_factors(h, par)
        col = jnp.concatenate([il] * 8, axis=0).T[:, 0:1]
        d = (qd[h, :, HD:].astype(F32) * col).astype(BF16)
        for m in range(0, keys, CHUNK):
            e = e_buf[slot, m : m + CHUNK]
            f = f_buf[slot, m : m + CHUNK].astype(F32)
            f_buf[slot, m : m + CHUNK] = (f * il - e.astype(F32) * w).astype(BF16)
            dv[m : m + CHUNK] += jnp.dot(e, d, preferred_element_type=F32)
        dq_part[h] = jnp.dot(kt[...], f_buf[slot], preferred_element_type=F32).T.astype(BF16)

    def key_grads(h):
        slot = lax.rem(h, SLOTS)
        q = qd[h, :, :HD]
        for m in range(0, keys, CHUNK):
            dk[m : m + CHUNK] += jnp.dot(f_buf[slot, m : m + CHUNK], q, preferred_element_type=F32)

    def step(s, par):
        odd = 1 - par

        def forward():
            @pl.when(s + 1 < DIRECT)
            def _():
                direct_bytes(s + 1).wait_recv()
                go(gather(s + 1, odd, 2))

            @pl.when((s + 1 >= DIRECT) & (s + 1 < heads))
            def _():
                advance(s + 1, odd, 1)

        @pl.when(s < heads)
        def _():
            gather_bytes(s, par, 2).wait_recv()
            first_pass(s, par, forward)
            stat(s).start()

        @pl.when((s + 2 >= DIRECT) & (s + 2 < heads))
        def _():
            advance(s + 2, par, 0)

        @pl.when((s + 3 >= DIRECT) & (s + 3 < heads))
        def _():
            go(gather(s + 3, odd, 0))

        @pl.when(s >= LAG)
        def _():
            stat_bytes(s - LAG).wait_recv()
            score_grads(s - LAG, par)
            reduce_sib(s - LAG).start()

        @pl.when(s < heads)
        def _():
            stat_spread(s)

        @pl.when(s >= LAG)
        def _():
            key_grads(s - LAG)
            reduce_first(s - LAG, par)

        @pl.when(s > LAG)
        def _():
            reduce_second(s - LAG - 1, odd)

    def pair(t, carry):
        step(2 * t, 0)
        step(2 * t + 1, 1)
        return carry

    lax.fori_loop(0, (heads + LAG) // 2, pair, 0)

    for h in range(heads - 2):
        finish(h)
    for t in range(heads):
        pltpu.make_async_copy(w_ref.at[pl.ds(t * cols, cols)], w_buf.at[t], w_sem.at[t]).wait()
    dv_out = pltpu.make_async_copy(dv, dv_ref, out_sem.at[0])
    dv_out.start()
    ready = (heads - 2) * HD

    def early(t):
        t_sum[t] = lax.dot_general(dq[:, :ready], w_buf[t, :, :ready], NT, preferred_element_type=F32)

    for t in range(8):
        early(t)
    k = k_ref[...].astype(F32)
    k_scale = lax.rsqrt(jnp.mean(k * k, axis=-1, keepdims=True) + EPS)
    g = dk[...] * kg_ref[...]
    dk[...] = k_scale * g - k * k_scale**3 * jnp.mean(k * g, axis=-1, keepdims=True)
    dk_out = pltpu.make_async_copy(dk, dk_ref, out_sem.at[1])
    dk_out.start()
    finish(heads - 2)
    finish(heads - 1)

    def text(k):
        return push(t_out.at[k], t_in.at[7 - k], tx_send.at[k], tx_recv.at[7 - k], {"head": group(k)})

    def term(to):
        late = lax.dot_general(dq[:, ready:], w_buf[to, :, ready:], NT, preferred_element_type=F32)
        return t_sum[to] + late

    for k in (3, 5, 4, 1, 7, 2, 6):
        t_out[k] = term(group(k)).astype(BF16)
        text(k).start()
    total = term(head)

    def drain(h, carry):
        stat(h).wait_send()
        stat_bytes(h).wait_send()
        reduce_sib(h).wait_send()
        gather_bytes(h, 0, 2).wait_send()
        return carry

    def drain_pair(t, carry):
        for par in range(2):
            h = 2 * t + par

            @pl.when(h < heads - 1)
            def _():
                reduce_bytes(h, par, 1).wait_send()
                reduce_bytes(h, par, 2).wait_send()

            @pl.when(h < DIRECT)
            def _():
                direct_bytes(h).wait_send()

            @pl.when(h >= DIRECT)
            def _():
                gather_bytes(h, par, 0).wait_send()
                gather_bytes(h, par, 1).wait_send()

        return carry

    lax.fori_loop(0, heads, drain, 0)
    lax.fori_loop(0, heads // 2, drain_pair, 0)
    last_bytes().wait_send()
    for k in (4, 2, 3, 6, 0, 5, 1):
        text(7 - k).wait_recv()
        total = total + t_in[k].astype(F32)
    text_ref[...] = total
    for k in range(1, 8):
        text(k).wait_send()
    dv_out.wait()
    dk_out.wait()


def copy_kernel(*refs):
    for src, dst in zip(refs[:3], refs[3:]):
        dst[...] = src[...]


def local(queries, q_gain, keys, k_gain, values, out_grad, w_query, span_mask, frame_len):
    rows, width = queries.shape
    heads = width // HD
    every = lax.axis_size("frame") * rows
    half = every // 2
    n = keys.shape[0]
    cols = w_query.shape[0] // lax.axis_size("head")
    vmem = pl.BlockSpec(memory_space=pltpu.VMEM)
    smem = pl.BlockSpec(memory_space=pltpu.SMEM)
    anywhere = pl.BlockSpec(memory_space=pl.ANY)
    stat = 2 * every // HD
    sems = pltpu.SemaphoreType.DMA
    results = pl.pallas_call(
        functools.partial(kernel, heads, rows),
        out_shape=(
            jax.ShapeDtypeStruct((rows, cols), F32),
            jax.ShapeDtypeStruct((n, HD), F32),
            jax.ShapeDtypeStruct((n, HD), F32),
        ),
        in_specs=[vmem] * 7 + [smem, anywhere],
        out_specs=(vmem, anywhere, anywhere),
        scratch_shapes=[
            pltpu.VMEM((heads, every, 2 * HD), BF16),
            pltpu.VMEM((SLOTS, n, every), BF16),
            pltpu.VMEM((SLOTS, n, every), BF16),
            pltpu.VMEM((n, HD), BF16),
            pltpu.VMEM((HD, n), BF16),
            pltpu.VMEM((n, HD), F32),
            pltpu.VMEM((2, 1, every), F32),
            pltpu.VMEM((n, HD), F32),
            pltpu.VMEM((n, HD), F32),
            pltpu.VMEM((heads, stat, HD), F32),
            pltpu.VMEM((heads, stat, HD), F32),
            pltpu.VMEM((heads, stat, HD), F32),
            pltpu.VMEM((heads, 8, stat, HD), F32),
            pltpu.VMEM((heads, every, HD), BF16),
            pltpu.VMEM((heads, half, HD), BF16),
            pltpu.VMEM((heads, half, HD), BF16),
            pltpu.VMEM((heads, 6 * rows, HD), BF16),
            pltpu.VMEM((heads, 4 * rows, HD), BF16),
            pltpu.VMEM((heads, 3 * rows, HD), BF16),
            pltpu.VMEM((7, rows, HD), BF16),
            pltpu.VMEM((rows, width), BF16),
            pltpu.VMEM((heads, cols, width), BF16),
            pltpu.VMEM((8, rows, cols), F32),
            pltpu.VMEM((8, rows, cols), BF16),
            pltpu.VMEM((8, rows, cols), BF16),
        ]
        + [sems((3, heads))] * 2
        + [sems((2, heads))] * 2
        + [sems((3, heads))] * 2
        + [sems((8,))] * 2
        + [sems((heads,)), sems((2,))],
        compiler_params=pltpu.CompilerParams(
            collective_id=0, has_side_effects=True, vmem_limit_bytes=62 * 2**20
        ),
        cost_estimate=pl.CostEstimate(
            flops=10 * heads * every * n * HD, bytes_accessed=2**25, transcendentals=heads * every * n
        ),
    )(
        queries, q_gain[None], keys, k_gain[None], values, out_grad, span_mask.reshape(1, -1), frame_len, w_query
    )
    return pl.pallas_call(
        copy_kernel,
        out_shape=[jax.ShapeDtypeStruct(a.shape, a.dtype) for a in results],
        in_specs=[vmem] * 3,
        out_specs=[vmem] * 3,
    )(*results)


def solution(mesh):
    return jax.shard_map(
        local,
        mesh=mesh,
        in_specs=(
            P("frame", "head"), P(), P("frame", "head"), P(), P("frame", "head"),
            P("frame", "head"), P(None, "head"), P(None, "frame"), P("frame"),
        ),
        out_specs=(P("frame", "head"), P("frame", "head"), P("frame", "head")),
        check_vma=False,
    )
```

```python
import functools

import jax
import jax.numpy as jnp
from jax import lax
from jax.experimental import pallas as pl
from jax.experimental.pallas import tpu as pltpu
from jax.sharding import PartitionSpec as P

MESH = pl.DeviceIdType.MESH
BLK = 16
EPS = 1e-05
HD = 128
LAG = 2
SLOTS = LAG + 1
CHUNK = 320
DIRECT = 4
F32 = jnp.float32
BF16 = jnp.bfloat16
NT = (((1,), (1,)), ((), ()))


def kernel(
    heads, rows, q_ref, qg_ref, k_ref, kg_ref, v_ref, d_ref, span_ref, len_ref, w_ref,
    text_ref, dk_ref, dv_ref,
    qd, e_buf, f_buf, kb, kt, km, rm, dk, dv, lu, lu_in, lu_chip, lu_all, dq_part, dq_in0, dq_s0, dq_in1, dq_s1,
    dq_in2, dq_last, dq, w_buf, t_sum, t_out, t_in,
    ag_send, ag_recv, st_send, st_recv, rs_send, rs_recv, tx_send, tx_recv, w_sem, out_sem,
):
    frame = lax.axis_index("frame")
    head = lax.axis_index("head")
    core = lax.rem(frame, 2)
    z = lax.rem(frame // 2, 4)
    x = frame // 8
    chip = frame // 2
    half = 8 * rows
    every = 2 * half
    keys = k_ref.shape[0]
    groups = every // HD
    cols = text_ref.shape[1]

    def frame_of(x_, z_, core_):
        return {"frame": x_ * 8 + z_ * 2 + core_}

    def around(k):
        return lax.rem(z + k, 4)

    sib = frame_of(x, z, 1 - core)
    x_near = frame_of(1 - x, z, core)

    def peer(k):
        return {"frame": 2 * lax.rem(chip + k, 8) + core}

    def group(k):
        return lax.rem(head + k, 8)

    def push(src, dst, send, recv, target):
        return pltpu.make_async_remote_copy(
            src_ref=src, dst_ref=dst, send_sem=send, recv_sem=recv, device_id=target, device_id_type=MESH
        )

    def span_of_rows(first, count, size):
        return pl.ds(pl.multiple_of(first, size), count)

    barrier = pltpu.get_barrier_semaphore()
    pl.semaphore_signal(barrier, inc=1, device_id=sib, device_id_type=MESH)
    for k in range(1, 8):
        pl.semaphore_signal(barrier, inc=1, device_id=peer(k), device_id_type=MESH)
        pl.semaphore_signal(barrier, inc=1, device_id={"head": group(k)}, device_id_type=MESH)

    def index(par, x_, z_):
        return x_ * 4 + z_ if par == 0 else z_ * 2 + x_

    def gather(h, par, stage):
        if stage == 2:
            block = qd.at[h, span_of_rows(core * half, half, half)]
            return [push(block, block, ag_send.at[2, h], ag_recv.at[2, h], sib)]
        if par == 0:
            first, blocks = ((index(0, x, z), 1), (x * 4, 4))[stage]
            along_z = stage == 0
        else:
            first, blocks = ((index(1, x, z), 1), (z * 2, 2))[stage]
            along_z = stage == 1
        block = qd.at[h, span_of_rows(core * half + first * rows, blocks * rows, rows)]
        targets = [frame_of(x, around(k), core) for k in (1, 2, 3)] if along_z else [x_near]
        return [push(block, block, ag_send.at[stage, h], ag_recv.at[stage, h], t) for t in targets]

    def gather_bytes(h, par, stage):
        count = (half, (3 * rows, 4 * rows), (rows, 6 * rows))[0 if stage == 2 else 1 + par]
        count = count if stage == 2 else count[stage]
        block = qd.at[h, pl.ds(0, count)]
        return push(block, block, ag_send.at[stage, h], ag_recv.at[stage, h], sib)

    def go(copies):
        for copy in copies:
            copy.start()

    def advance(h, par, stage):
        gather_bytes(h, par, stage).wait_recv()
        go(gather(h, par, stage + 1))

    def head_rows(h):
        at = slice(h * HD, (h + 1) * HD)
        mine = span_of_rows(core * half + index(h % 2, x, z) * rows, rows, rows)
        q = q_ref[:, at].astype(F32)
        scale = lax.rsqrt(jnp.mean(q * q, axis=-1, keepdims=True) + EPS)
        qd[h, mine, :HD] = (q * scale * qg_ref[...] * HD ** (-0.5)).astype(BF16)
        qd[h, mine, HD:] = d_ref[:, at]

    def direct(h, par, k):
        block = qd.at[h, span_of_rows(core * half + index(par, x, z) * rows, rows, rows)]
        return push(block, block, ag_send.at[0, h], ag_recv.at[0, h], peer(k))

    def direct_bytes(h):
        block = qd.at[h, pl.ds(0, 7 * rows)]
        return push(block, block, ag_send.at[0, h], ag_recv.at[0, h], sib)

    head_rows(0)
    pl.semaphore_wait(barrier, 15)
    for h in range(heads):
        if h > 0:
            head_rows(h)
        if h < DIRECT:
            for k in range(1, 8):
                direct(h, h % 2, k).start()
    for t in range(heads):
        pltpu.make_async_copy(w_ref.at[pl.ds(t * cols, cols)], w_buf.at[t], w_sem.at[t]).start()

    k = k_ref[...].astype(F32)
    k_scale = lax.rsqrt(jnp.mean(k * k, axis=-1, keepdims=True) + EPS)
    k = k * k_scale * kg_ref[...]
    kb[...] = k.astype(BF16)
    kt[...] = k.T.astype(BF16)
    km[...] = (lax.broadcasted_iota(jnp.int32, km.shape, 0) < len_ref[0]).astype(F32)
    spans = span_ref.shape[1]
    r = lax.broadcasted_iota(jnp.int32, (spans, every), 1)
    i = (r // rows) % 8
    for par in range(2):
        chip_of = i if par == 0 else (i % 2) * 4 + i // 2
        span_of = (chip_of * 2 + r // half) * (rows // BLK) + (r % rows) // BLK
        hit = (span_of == lax.broadcasted_iota(jnp.int32, r.shape, 0)).astype(F32)
        seen = jnp.broadcast_to((span_ref[...] > 0).astype(F32), (8, spans))
        rm[par] = jnp.dot(seen, hit, preferred_element_type=F32)[0:1]
    dk[...] = jnp.zeros_like(dk)
    dv[...] = jnp.zeros_like(dv)
    direct_bytes(0).wait_recv()
    go(gather(0, 0, 2))

    def stat(h):
        return push(lu.at[h], lu_in.at[h], st_send.at[0, h], st_recv.at[0, h], sib)

    def stat_out(h, k):
        return push(lu_chip.at[h], lu_all.at[h, chip], st_send.at[1, h], st_recv.at[1, h], peer(k))

    def stat_bytes(h):
        block = lu_all.at[h, pl.ds(0, 7)]
        return push(block, block, st_send.at[1, h], st_recv.at[1, h], sib)

    def stat_spread(h):
        stat(h).wait_recv()
        both = lu[h] + lu_in[h]
        lu_chip[h] = both
        lu_all[h, chip] = both
        for k in range(1, 8):
            stat_out(h, k).start()

    def reduce_sib(h):
        src = dq_part.at[h, span_of_rows((1 - core) * half, half, half)]
        return push(src, dq_in0.at[h], rs_send.at[0, h], rs_recv.at[0, h], sib)

    def reduce(h, par, stage):
        if par == 0 and stage == 1:
            src = dq_s0.at[h, span_of_rows((1 - x) * 4 * rows, 4 * rows, 4 * rows)]
            return [push(src, dq_in1.at[h, pl.ds(0, 4 * rows)], rs_send.at[1, h], rs_recv.at[1, h], x_near)]
        if par == 1 and stage == 2:
            src = dq_s1.at[h, span_of_rows((1 - x) * rows, rows, rows)]
            return [push(src, dq_in2.at[h, pl.ds(0, rows)], rs_send.at[2, h], rs_recv.at[2, h], x_near)]
        copies = []
        for k in (1, 2, 3):
            to = around(k)
            if par == 0:
                src = dq_s1.at[h, span_of_rows(to * rows, rows, rows)]
                dst = dq_in2.at[h, pl.ds((3 - k) * rows, rows)]
            else:
                src = dq_s0.at[h, span_of_rows(to * 2 * rows, 2 * rows, 2 * rows)]
                dst = dq_in1.at[h, pl.ds((3 - k) * 2 * rows, 2 * rows)]
            copies.append(push(src, dst, rs_send.at[stage, h], rs_recv.at[stage, h], frame_of(x, to, core)))
        return copies

    def reduce_bytes(h, par, stage):
        count = ((4, 3), (6, 1))[par][stage - 1] * rows
        block = (dq_in1 if stage == 1 else dq_in2).at[h, pl.ds(0, count)]
        return push(block, block, rs_send.at[stage, h], rs_recv.at[stage, h], sib)

    def last(par, k):
        h = heads - 2 + par
        to = lax.rem(chip + k, 8)
        src = dq_s0.at[h, span_of_rows(index(par, to // 4, lax.rem(to, 4)) * rows, rows, rows)]
        return push(src, dq_last.at[par, 7 - k], rs_send.at[1, h], rs_recv.at[1, h], peer(k))

    def last_bytes(par):
        block = dq_last.at[par, pl.ds(0, 7)]
        h = heads - 2 + par
        return push(block, block, rs_send.at[1, h], rs_recv.at[1, h], sib)

    def reduce_first(h, par):
        reduce_sib(h).wait_recv()
        own = dq_part[h, span_of_rows(core * half, half, half)]
        dq_s0[h] = (own.astype(F32) + dq_in0[h].astype(F32)).astype(BF16)

        @pl.when(h < heads - 2)
        def _():
            go(reduce(h, par, 1))

        @pl.when(h >= heads - 2)
        def _():
            for k in range(1, 8):
                last(par, k).start()

    def reduce_second(h, par):
        reduce_bytes(h, par, 1).wait_recv()
        if par == 0:
            own = dq_s0[h, span_of_rows(x * 4 * rows, 4 * rows, 4 * rows)].astype(F32)
            dq_s1[h] = (own + dq_in1[h, : 4 * rows].astype(F32)).astype(BF16)
        else:
            total = dq_s0[h, span_of_rows(z * 2 * rows, 2 * rows, 2 * rows)].astype(F32)
            for k in range(3):
                total = total + dq_in1[h, k * 2 * rows : (k + 1) * 2 * rows].astype(F32)
            dq_s1[h, : 2 * rows] = total.astype(BF16)
        go(reduce(h, par, 2))

    def finish(h):
        par = h % 2
        if h >= heads - 2:
            last_bytes(par).wait_recv()
            total = dq_s0[h, span_of_rows(index(par, x, z) * rows, rows, rows)].astype(F32)
            for k in range(7):
                total = total + dq_last[par, k].astype(F32)
        else:
            reduce_bytes(h, par, 2).wait_recv()
            mine = z if par == 0 else x
            total = dq_s1[h, span_of_rows(mine * rows, rows, rows)].astype(F32)
            for k in range(3 if par == 0 else 1):
                total = total + dq_in2[h, k * rows : (k + 1) * rows].astype(F32)
        at = slice(h * HD, (h + 1) * HD)
        q = q_ref[:, at].astype(F32)
        scale = lax.rsqrt(jnp.mean(q * q, axis=-1, keepdims=True) + EPS)
        g = total * HD ** (-0.5) * qg_ref[...]
        g = scale * g - q * scale**3 * jnp.mean(q * g, axis=-1, keepdims=True)
        dq[:, at] = g.astype(BF16)

    def first_pass(h, par, between):
        slot = lax.rem(h, SLOTS)
        q, d = qd[h, :, :HD], qd[h, :, HD:]
        l = jnp.zeros((1, every), F32)
        u = jnp.zeros((1, every), F32)
        for m in range(0, keys, CHUNK):
            s = lax.dot_general(kb[m : m + CHUNK], q, NT, preferred_element_type=F32)
            dp = lax.dot_general(v_ref[m : m + CHUNK], d, NT, preferred_element_type=F32)
            live = jnp.concatenate([km[m : m + CHUNK]] * groups, axis=1)
            e = jnp.exp(s) * live
            f = e * dp
            e_buf[slot, m : m + CHUNK] = e.astype(BF16)
            f_buf[slot, m : m + CHUNK] = f.astype(BF16)
            l += jnp.sum(e, axis=0, keepdims=True)
            u += jnp.sum(f, axis=0, keepdims=True)
            if m == 2 * CHUNK:
                between()
        l *= rm[par]
        u *= rm[par]
        for j in range(groups):
            lu[h, j : j + 1] = l[:, j * HD : (j + 1) * HD]
            lu[h, groups + j : groups + j + 1] = u[:, j * HD : (j + 1) * HD]

    def row_factors(h, par):
        total = lu_all[h, 0]
        for c in range(1, 8):
            total = total + lu_all[h, c]
        l = jnp.concatenate([total[j : j + 1] for j in range(groups)], axis=1)
        u = jnp.concatenate([total[groups + j : groups + j + 1] for j in range(groups)], axis=1)
        il = rm[par] / l
        return il, (u / l) * il

    def second_pass(h, par):
        slot = lax.rem(h, SLOTS)
        il, w = row_factors(h, par)
        col = jnp.concatenate([il] * 8, axis=0).T[:, 0:1]
        d = (qd[h, :, HD:].astype(F32) * col).astype(BF16)
        for m in range(0, keys, CHUNK):
            e = e_buf[slot, m : m + CHUNK]
            f = f_buf[slot, m : m + CHUNK].astype(F32)
            f_buf[slot, m : m + CHUNK] = (f * il - e.astype(F32) * w).astype(BF16)
            dv[m : m + CHUNK] += jnp.dot(e, d, preferred_element_type=F32)
        dqt = jnp.dot(kt[...], f_buf[slot], preferred_element_type=F32)
        q = qd[h, :, :HD]
        for m in range(0, keys, CHUNK):
            dk[m : m + CHUNK] += jnp.dot(f_buf[slot, m : m + CHUNK], q, preferred_element_type=F32)
        dq_part[h] = dqt.T.astype(BF16)

    def step(s, par):
        odd = 1 - par

        def forward():
            @pl.when(s + 1 < DIRECT)
            def _():
                direct_bytes(s + 1).wait_recv()
                go(gather(s + 1, odd, 2))

            @pl.when((s + 1 >= DIRECT) & (s + 1 < heads))
            def _():
                advance(s + 1, odd, 1)

        @pl.when(s < heads)
        def _():
            gather_bytes(s, par, 2).wait_recv()
            first_pass(s, par, forward)
            stat(s).start()

        @pl.when((s + 2 >= DIRECT) & (s + 2 < heads))
        def _():
            advance(s + 2, par, 0)

        @pl.when((s + 3 >= DIRECT) & (s + 3 < heads))
        def _():
            go(gather(s + 3, odd, 0))

        @pl.when(s > LAG)
        def _():
            reduce_first(s - LAG - 1, odd)

        @pl.when(s > LAG + 1)
        def _():
            reduce_second(s - LAG - 2, par)

        @pl.when(s >= LAG)
        def _():
            stat_bytes(s - LAG).wait_recv()
            second_pass(s - LAG, par)
            reduce_sib(s - LAG).start()

        @pl.when(s < heads)
        def _():
            stat_spread(s)

    def pair(t, carry):
        step(2 * t, 0)
        step(2 * t + 1, 1)
        return carry

    lax.fori_loop(0, (heads + LAG) // 2, pair, 0)

    for h in range(heads - 2):
        finish(h)
    for t in range(heads):
        pltpu.make_async_copy(w_ref.at[pl.ds(t * cols, cols)], w_buf.at[t], w_sem.at[t]).wait()
    dv_out = pltpu.make_async_copy(dv, dv_ref, out_sem.at[0])
    dv_out.start()
    ready = (heads - 2) * HD

    def early(t):
        t_sum[t] = lax.dot_general(dq[:, :ready], w_buf[t, :, :ready], NT, preferred_element_type=F32)

    early(0)
    reduce_first(heads - 1, 1)
    for t in range(1, 8):
        early(t)
    k = k_ref[...].astype(F32)
    k_scale = lax.rsqrt(jnp.mean(k * k, axis=-1, keepdims=True) + EPS)
    g = dk[...] * kg_ref[...]
    dk[...] = k_scale * g - k * k_scale**3 * jnp.mean(k * g, axis=-1, keepdims=True)
    dk_out = pltpu.make_async_copy(dk, dk_ref, out_sem.at[1])
    dk_out.start()
    finish(heads - 2)
    finish(heads - 1)

    def text(k):
        return push(t_out.at[k], t_in.at[7 - k], tx_send.at[k], tx_recv.at[7 - k], {"head": group(k)})

    def term(to):
        late = lax.dot_general(dq[:, ready:], w_buf[to, :, ready:], NT, preferred_element_type=F32)
        return t_sum[to] + late

    for k in (3, 5, 4, 1, 7, 2, 6):
        t_out[k] = term(group(k)).astype(BF16)
        text(k).start()
    total = term(head)

    def drain(h, carry):
        stat(h).wait_send()
        stat_bytes(h).wait_send()
        reduce_sib(h).wait_send()
        gather_bytes(h, 0, 2).wait_send()
        return carry

    def drain_pair(t, carry):
        for par in range(2):
            h = 2 * t + par

            @pl.when(h < heads - 2)
            def _():
                reduce_bytes(h, par, 1).wait_send()
                reduce_bytes(h, par, 2).wait_send()

            @pl.when(h < DIRECT)
            def _():
                direct_bytes(h).wait_send()

            @pl.when(h >= DIRECT)
            def _():
                gather_bytes(h, par, 0).wait_send()
                gather_bytes(h, par, 1).wait_send()

        return carry

    lax.fori_loop(0, heads, drain, 0)
    lax.fori_loop(0, heads // 2, drain_pair, 0)
    last_bytes(0).wait_send()
    last_bytes(1).wait_send()
    for k in (4, 2, 3, 6, 0, 5, 1):
        text(7 - k).wait_recv()
        total = total + t_in[k].astype(F32)
    text_ref[...] = total
    for k in range(1, 8):
        text(k).wait_send()
    dv_out.wait()
    dk_out.wait()


def copy_kernel(*refs):
    for src, dst in zip(refs[:3], refs[3:]):
        dst[...] = src[...]


def local(queries, q_gain, keys, k_gain, values, out_grad, w_query, span_mask, frame_len):
    rows, width = queries.shape
    heads = width // HD
    every = lax.axis_size("frame") * rows
    half = every // 2
    n = keys.shape[0]
    cols = w_query.shape[0] // lax.axis_size("head")
    vmem = pl.BlockSpec(memory_space=pltpu.VMEM)
    smem = pl.BlockSpec(memory_space=pltpu.SMEM)
    anywhere = pl.BlockSpec(memory_space=pl.ANY)
    stat = 2 * every // HD
    sems = pltpu.SemaphoreType.DMA
    results = pl.pallas_call(
        functools.partial(kernel, heads, rows),
        out_shape=(
            jax.ShapeDtypeStruct((rows, cols), F32),
            jax.ShapeDtypeStruct((n, HD), F32),
            jax.ShapeDtypeStruct((n, HD), F32),
        ),
        in_specs=[vmem] * 7 + [smem, anywhere],
        out_specs=(vmem, anywhere, anywhere),
        scratch_shapes=[
            pltpu.VMEM((heads, every, 2 * HD), BF16),
            pltpu.VMEM((SLOTS, n, every), BF16),
            pltpu.VMEM((SLOTS, n, every), BF16),
            pltpu.VMEM((n, HD), BF16),
            pltpu.VMEM((HD, n), BF16),
            pltpu.VMEM((n, HD), F32),
            pltpu.VMEM((2, 1, every), F32),
            pltpu.VMEM((n, HD), F32),
            pltpu.VMEM((n, HD), F32),
            pltpu.VMEM((heads, stat, HD), F32),
            pltpu.VMEM((heads, stat, HD), F32),
            pltpu.VMEM((heads, stat, HD), F32),
            pltpu.VMEM((heads, 8, stat, HD), F32),
            pltpu.VMEM((heads, every, HD), BF16),
            pltpu.VMEM((heads, half, HD), BF16),
            pltpu.VMEM((heads, half, HD), BF16),
            pltpu.VMEM((heads, 6 * rows, HD), BF16),
            pltpu.VMEM((heads, 4 * rows, HD), BF16),
            pltpu.VMEM((heads, 3 * rows, HD), BF16),
            pltpu.VMEM((2, 7, rows, HD), BF16),
            pltpu.VMEM((rows, width), BF16),
            pltpu.VMEM((heads, cols, width), BF16),
            pltpu.VMEM((8, rows, cols), F32),
            pltpu.VMEM((8, rows, cols), BF16),
            pltpu.VMEM((8, rows, cols), BF16),
        ]
        + [sems((3, heads))] * 2
        + [sems((2, heads))] * 2
        + [sems((3, heads))] * 2
        + [sems((8,))] * 2
        + [sems((heads,)), sems((2,))],
        compiler_params=pltpu.CompilerParams(
            collective_id=0, has_side_effects=True, vmem_limit_bytes=62 * 2**20
        ),
        cost_estimate=pl.CostEstimate(
            flops=10 * heads * every * n * HD, bytes_accessed=2**25, transcendentals=heads * every * n
        ),
    )(
        queries, q_gain[None], keys, k_gain[None], values, out_grad, span_mask.reshape(1, -1), frame_len, w_query
    )
    return pl.pallas_call(
        copy_kernel,
        out_shape=[jax.ShapeDtypeStruct(a.shape, a.dtype) for a in results],
        in_specs=[vmem] * 3,
        out_specs=[vmem] * 3,
    )(*results)


def solution(mesh):
    return jax.shard_map(
        local,
        mesh=mesh,
        in_specs=(
            P("frame", "head"), P(), P("frame", "head"), P(), P("frame", "head"),
            P("frame", "head"), P(None, "head"), P(None, "frame"), P("frame"),
        ),
        out_specs=(P("frame", "head"), P("frame", "head"), P("frame", "head")),
        check_vma=False,
    )
```
